32 devices in a mesh: blk: 32 (over z, y, x, core).
Axes of the slice: x: 2, y: 2, z: 4, core: 2. Of those that a mesh axis runs over, the one named last changes fastest.
Arguments:
- populations: float32 [2048, 19, 128], P('blk'), may hold values from 0 to 1, as said below
- relax_rates: float32 [19], replicated, may hold values from 0.6 to 1.8
- destination: int32 [2048], P('blk'), may hold values from 0 to 2559, as said below
- block_links: int32 [2560, 18], P('blk'), may hold values from -1 to 2559, as said below
- site_flags: int32 [2560, 128], P('blk'), may hold values from 0 to 3, as said below
Outputs:
- current: float32 [2560, 19, 128], P('blk')
The draws below stay inside these ranges and needn't reach their ends.
Inputs may be any that keep to these rules, and one draw needn't show every extreme that they name: `destination`: old positions are in the vessel's geometric order: block g lies in layer g // 16. After the repartition each owner's blocks are consecutive in that order and fill its slots from slot 0 in the same order; only an owner's last blocks leave it, all to the next owner, at most 16 of them; in every draw some owner sends 16 and the next one sends none, so that it holds 80 blocks; every owner holds 48 or more. `block_links`: entry n of an occupied slot's row is the new position of the neighbouring block in direction n, or -1 where the vessel has none; links are mutual; a neighbour lies in the same layer or an adjacent one; rows of empty slots are all -1. `site_flags`: 0 fluid, 1 wall (every site of an empty slot too), 2 inlet, 3 outlet. `populations`: Positive, below the weights times two.
All inputs are finite; a program needn't handle non-finite values.
Results may differ from the reference program's by a relative error of at most 0.0003.
Values sent between devices are 32-bit elements; how exact they have to be, the bound alone decides.
A program may use at most 64 MiB of HBM per device.

```python
import jax
import jax.numpy as jnp
import numpy as np
from jax import lax

Q = 19
SITES = 128
SIDE = 4
BPD = 64
STEPS = 2
LAYER = 16
MOVE = 16
CAP = 80
BLOCKS = 2048
SLOTS = 2560
LAYERS = 128
N_BLK = 32


def offset_list():
    found = []
    for along_x in (-1, 0, 1):
        for along_y in (-1, 0, 1):
            for along_z in (-1, 0, 1):
                if 1 <= abs(along_x) + abs(along_y) + abs(along_z) <= 2:
                    found.append((along_x, along_y, along_z))
    return np.array(found, dtype=np.int32)


def weight_list():
    offsets = offset_list()
    lengths = np.concatenate([np.zeros(1, np.int32), np.sum(offsets * offsets, axis=1)])
    return np.where(lengths == 0, 1.0 / 3.0, np.where(lengths == 1, 1.0 / 18.0, 1.0 / 36.0)).astype(np.float32)


def block_layout(key):
    departing = jax.random.randint(jax.random.fold_in(key, 101), (N_BLK,), 0, MOVE + 1)
    chosen = jax.random.randint(jax.random.fold_in(key, 102), (), 0, N_BLK - 1)
    owners = jnp.arange(N_BLK)
    departing = jnp.where(owners == chosen, MOVE, departing)
    departing = jnp.where(owners == chosen + 1, 0, departing)
    departing = jnp.where(owners == N_BLK - 1, 0, departing)
    earlier = jnp.concatenate([jnp.zeros((1,), departing.dtype), departing[:-1]])
    position = jnp.arange(BLOCKS)
    old_owner = position // BPD
    old_slot = position % BPD
    leaving = old_slot >= BPD - departing[old_owner]
    new_owner = jnp.where(leaving, old_owner + 1, old_owner)
    new_slot = jnp.where(leaving, old_slot - (BPD - departing[old_owner]), old_slot + earlier[old_owner])
    return (new_owner * CAP + new_slot).astype(jnp.int32)


def layer_orders(key):
    scores = jax.random.randint(jax.random.fold_in(key, 103), (LAYERS, LAYER), 0, 1 << 20) * LAYER + jnp.arange(LAYER)[None, :]
    cell_order = jnp.argsort(scores, axis=1)
    inverse = jnp.argsort(cell_order, axis=1)
    return (cell_order, inverse)


def draw_destination(key, part):
    layout = block_layout(key)
    return layout


def draw_block_links(key, part):
    layout = block_layout(key)
    cell_order, inverse = layer_orders(key)
    position = jnp.arange(BLOCKS)
    layer_index = position // LAYER
    cell_index = cell_order[layer_index, position % LAYER]
    offsets = jnp.asarray(offset_list())
    target_x = (cell_index // SIDE)[:, None] + offsets[None, :, 0]
    target_y = (cell_index % SIDE)[:, None] + offsets[None, :, 1]
    target_layer = layer_index[:, None] + offsets[None, :, 2]
    inside = (target_x >= 0) & (target_x < SIDE) & (target_y >= 0) & (target_y < SIDE) & (target_layer >= 0) & (target_layer < LAYERS)
    clipped_layer = jnp.clip(target_layer, 0, LAYERS - 1)
    target_cell = jnp.clip(target_x, 0, SIDE - 1) * SIDE + jnp.clip(target_y, 0, SIDE - 1)
    target_position = clipped_layer * LAYER + inverse[clipped_layer, target_cell]
    link_rows = jnp.where(inside, layout[target_position], -1).astype(jnp.int32)
    return jnp.full((SLOTS, 18), -1, jnp.int32).at[layout].set(link_rows)


def draw_site_flags(key, part):
    layout = block_layout(key)
    key = jax.random.fold_in(key, 5)
    wall_site = jax.random.randint(key, (BLOCKS, SITES), 0, 8) == 0
    layer_index = (jnp.arange(BLOCKS) // LAYER)[:, None]
    depth_index = (jnp.arange(SITES) % 8)[None, :]
    site_kind = jnp.where(wall_site, 1, 0)
    site_kind = jnp.where((layer_index == 0) & (depth_index == 0), 2, site_kind)
    site_kind = jnp.where((layer_index == LAYERS - 1) & (depth_index == 7), 3, site_kind)
    return jnp.full((SLOTS, SITES), 1, jnp.int32).at[layout].set(site_kind.astype(jnp.int32))


def draw_populations(key, part):
    key = jax.random.fold_in(key, 9)
    weights = jnp.asarray(weight_list(), jnp.float32)[None, :, None]
    spread = jax.random.uniform(key, (BLOCKS, Q, SITES), jnp.float32)
    return weights * (0.3 + 1.4 * spread)


def setup_inputs(seed: int = 0) -> dict:
    streams_of = jax.random.split(jax.random.key(seed), 6)
    populations = draw_populations(jax.random.fold_in(streams_of[5], 71), 0)
    relax_rates = jnp.clip(jax.random.uniform(streams_of[1], (Q,), jnp.float32, 0.6, 1.8), 0.6, 1.8)
    destination = draw_destination(jax.random.fold_in(streams_of[5], 71), 0)
    block_links = draw_block_links(jax.random.fold_in(streams_of[5], 71), 0)
    site_flags = draw_site_flags(jax.random.fold_in(streams_of[5], 71), 0)
    return dict(populations=populations, relax_rates=relax_rates, destination=destination, block_links=block_links, site_flags=site_flags)


INLET_SPEED = 0.05


def offset_table():
    found = []
    for along_x in (-1, 0, 1):
        for along_y in (-1, 0, 1):
            for along_z in (-1, 0, 1):
                if 1 <= abs(along_x) + abs(along_y) + abs(along_z) <= 2:
                    found.append((along_x, along_y, along_z))
    return np.array(found, dtype=np.int32)


def velocity_table():
    return np.concatenate([np.zeros((1, 3), np.int32), offset_table()], 0)


def weight_table():
    velocities = velocity_table()
    lengths = np.sum(velocities * velocities, axis=1)
    return np.where(lengths == 0, 1.0 / 3.0, np.where(lengths == 1, 1.0 / 18.0, 1.0 / 36.0)).astype(np.float32)


def opposite_table():
    velocities = velocity_table()
    found = []
    for velocity in range(19):
        for mirror in range(19):
            if np.all(velocities[mirror] == -velocities[velocity]):
                found.append(mirror)
    return np.array(found, dtype=np.int32)


def moment_table():
    velocities = velocity_table()
    speed_x = velocities[:, 0].astype(np.float32)
    speed_y = velocities[:, 1].astype(np.float32)
    speed_z = velocities[:, 2].astype(np.float32)
    energy = speed_x * speed_x + speed_y * speed_y + speed_z * speed_z
    factor = 5.0 * energy - 9.0
    stress = 3.0 * energy - 5.0
    normal_xx = 3.0 * speed_x * speed_x - energy
    normal_ww = speed_y * speed_y - speed_z * speed_z
    lines = [np.ones(19, np.float32), 19.0 * energy - 30.0, (21.0 * energy * energy - 53.0 * energy + 24.0) / 2.0,
             speed_x, factor * speed_x, speed_y, factor * speed_y, speed_z, factor * speed_z,
             normal_xx, stress * normal_xx, normal_ww, stress * normal_ww,
             speed_x * speed_y, speed_y * speed_z, speed_x * speed_z,
             (speed_y * speed_y - speed_z * speed_z) * speed_x,
             (speed_z * speed_z - speed_x * speed_x) * speed_y,
             (speed_x * speed_x - speed_y * speed_y) * speed_z]
    return np.stack(lines, 0).astype(np.float32)


def moment_inverse():
    matrix = moment_table()
    return (matrix / np.sum(matrix * matrix, axis=1, keepdims=True)).T.astype(np.float32)


def region_table():
    velocities = velocity_table()
    offsets = offset_table()
    table = np.full((19, 128), -1, dtype=np.int32)
    for velocity in range(19):
        for site in range(128):
            upstream_x = site // 32 - int(velocities[velocity, 0])
            upstream_y = (site // 8) % 4 - int(velocities[velocity, 1])
            upstream_z = site % 8 - int(velocities[velocity, 2])
            block_step = (upstream_x // 4, upstream_y // 4, upstream_z // 8)
            if block_step != (0, 0, 0):
                for direction in range(18):
                    if tuple(int(entry) for entry in offsets[direction]) == block_step:
                        table[velocity, site] = direction
    return table


def equilibrium(density, momentum):
    velocity = jnp.asarray(velocity_table(), jnp.float32)
    weights = jnp.asarray(weight_table(), jnp.float32)
    projected = jnp.einsum("qd,bds->bqs", velocity, momentum, precision=lax.Precision.HIGHEST)
    square = jnp.sum(momentum * momentum, axis=1)
    return weights[None, :, None] * (density[:, None, :] + 3.0 * projected + 4.5 * projected * projected - 1.5 * square[:, None, :])


def collide(populations, site_flags, relax_rates):
    highest = lax.Precision.HIGHEST
    velocity = jnp.asarray(velocity_table(), jnp.float32)
    density = jnp.sum(populations, axis=1)
    momentum = jnp.einsum("bqs,qd->bds", populations, velocity, precision=highest)
    relaxation = jnp.dot(jnp.asarray(moment_inverse(), jnp.float32) * relax_rates[None, :], jnp.asarray(moment_table(), jnp.float32), precision=highest)
    relaxed = populations - jnp.einsum("qr,brs->bqs", relaxation, populations - equilibrium(density, momentum), precision=highest)
    bounced = populations[:, opposite_table(), :]
    unit_density = jnp.ones_like(density)
    inflow = jnp.zeros_like(momentum).at[:, 2, :].set(INLET_SPEED)
    inlet_eq = equilibrium(unit_density, inflow)
    outlet = equilibrium(unit_density, momentum)
    site_kind = site_flags[:, None, :]
    return jnp.where(site_kind == 0, relaxed, jnp.where(site_kind == 1, bounced, jnp.where(site_kind == 2, inlet_eq, outlet)))


def propagate(collided, source, source_index):
    velocities = velocity_table()
    opposites = opposite_table()
    regions = region_table()
    result = [collided[:, 0, :]]
    for velocity in range(1, 19):
        shift_x = int(velocities[velocity, 0])
        shift_y = int(velocities[velocity, 1])
        shift_z = int(velocities[velocity, 2])

        def rolled(sheet):
            tile_cube = sheet.reshape(sheet.shape[0], 4, 4, 8)
            return jnp.roll(tile_cube, (shift_x, shift_y, shift_z), axis=(1, 2, 3)).reshape(sheet.shape[0], 128)

        moved = rolled(collided[:, velocity, :])
        reflected = collided[:, int(opposites[velocity]), :]
        region = regions[velocity]
        for direction in sorted(set(int(entry) for entry in region) - {-1}):
            neighbour_rows = source_index[:, direction]
            present = neighbour_rows >= 0
            fetched = jnp.take(source[:, velocity, :], jnp.maximum(neighbour_rows, 0), axis=0)
            remote = jnp.where(present[:, None], rolled(fetched), reflected)
            moved = jnp.where(jnp.asarray(region == direction)[None, :], remote, moved)
        result.append(moved)
    return jnp.stack(result, axis=1)


def reference(populations, relax_rates, destination, block_links, site_flags):
    current = jnp.zeros((SLOTS, Q, SITES), jnp.float32).at[destination].set(populations)
    flag_groups = site_flags.reshape(N_BLK, CAP, SITES)
    for iteration in range(STEPS):
        grouped = current.reshape(N_BLK, CAP, Q, SITES)
        collided = lax.map(lambda grouping: collide(grouping[0], grouping[1], relax_rates), (grouped, flag_groups))
        collided = collided.reshape(SLOTS, Q, SITES)
        current = propagate(collided, collided, block_links)
    return current
```

```python
import functools

import jax
import jax.numpy as jnp
import numpy as np
from jax import lax
from jax.experimental import pallas as pl
from jax.experimental.pallas import tpu as pltpu
from jax.sharding import PartitionSpec as P

Q = 19
SITES = 128
LAYER = 16
INLET_SPEED = 0.05
CHUNK = 16
MESH = pl.DeviceIdType.MESH

OFFSETS = [
    (x, y, z)
    for x in (-1, 0, 1)
    for y in (-1, 0, 1)
    for z in (-1, 0, 1)
    if 1 <= abs(x) + abs(y) + abs(z) <= 2
]
VELOCITIES = [(0, 0, 0)] + OFFSETS
WEIGHTS = [(1 / 3, 1 / 18, 1 / 36)[sum(abs(e) for e in c)] for c in VELOCITIES]
INDEX = {c: q for q, c in enumerate(VELOCITIES)}
PAIRS = [q for q in range(10, 19)]


def moment_norms():
    c = np.array(VELOCITIES, np.float64)
    x, y, z = c.T
    e = x * x + y * y + z * z
    f = 5 * e - 9
    s = 3 * e - 5
    xx = 3 * x * x - e
    ww = y * y - z * z
    rows = [
        np.ones(19), 19 * e - 30, (21 * e * e - 53 * e + 24) / 2, x, f * x, y, f * y, z, f * z,
        xx, s * xx, ww, s * ww, x * y, y * z, x * z,
        (y * y - z * z) * x, (z * z - x * x) * y, (x * x - y * y) * z,
    ]
    return [float(np.sum(r * r)) for r in rows]


NORMS = moment_norms()


def regions_of(q):
    cx, cy, cz = VELOCITIES[q]
    found = []
    for nx in sorted({0, -cx}):
        for ny in sorted({0, -cy}):
            for nz in sorted({0, -cz}):
                if (nx, ny, nz) == (0, 0, 0):
                    continue
                shift = (32 * cx + 8 * cy + cz + 32 * ny + 8 * nz) % SITES
                found.append((INDEX[(nx, ny, nz)] - 1, (nx, ny, nz), shift))
    return found


def lane_region(q, step, lane):
    cx, cy, cz = VELOCITIES[q]
    mask = None
    for c, n, value, side in (
        (cx, step[0], lane // 32, 4),
        (cy, step[1], (lane // 8) % 4, 4),
        (cz, step[2], lane % 8, 8),
    ):
        if c == 0:
            continue
        edge = 0 if c > 0 else side - 1
        part = (value == edge) if n != 0 else (value != edge)
        mask = part if mask is None else jnp.logical_and(mask, part)
    return mask


def rolled(value, shift):
    return value if shift % SITES == 0 else pltpu.roll(value, shift % SITES, 1)


def combos(get, jx, jy, jz):
    return {
        (0, 0, 1): jz, (0, 1, 0): jy, (1, 0, 0): jx,
        (0, 1, 1): jy + jz, (0, 1, -1): jy - jz,
        (1, 0, 1): jx + jz, (1, 0, -1): jx - jz,
        (1, 1, 0): jx + jy, (1, -1, 0): jx - jy,
    }


def odd_sums(a):
    x1 = a[(1, 1, 0)] + a[(1, -1, 0)]
    x2 = a[(1, 0, 1)] + a[(1, 0, -1)]
    y1 = a[(1, 1, 0)] - a[(1, -1, 0)]
    y2 = a[(0, 1, 1)] + a[(0, 1, -1)]
    z1 = a[(1, 0, 1)] - a[(1, 0, -1)]
    z2 = a[(0, 1, 1)] - a[(0, 1, -1)]
    return x1, x2, y1, y2, z1, z2


def collide(f, kind, rate):
    pos = [VELOCITIES[q] for q in PAIRS]
    weight = {c: WEIGHTS[INDEX[c]] for c in pos}
    s = {c: f[INDEX[c]] + f[19 - INDEX[c]] for c in pos}
    a = {c: f[INDEX[c]] - f[19 - INDEX[c]] for c in pos}
    density = f[0]
    for c in pos:
        density = density + s[c]
    x1, x2, y1, y2, z1, z2 = odd_sums(a)
    jx = a[(1, 0, 0)] + x1 + x2
    jy = a[(0, 1, 0)] + y1 + y2
    jz = a[(0, 0, 1)] + z1 + z2
    cj = combos(None, jx, jy, jz)
    square = 1.5 * (jx * jx + jy * jy + jz * jz)
    outlet_base = 1.0 - square
    fluid_base = density - square
    quad = {c: 4.5 * (cj[c] * cj[c]) for c in pos}
    d0 = f[0] - WEIGHTS[0] * fluid_base
    ds = {c: s[c] - (2 * weight[c]) * (fluid_base + quad[c]) for c in pos}
    da = {c: a[c] - (6 * weight[c]) * cj[c] for c in pos}
    ax, ay, az = ds[(1, 0, 0)], ds[(0, 1, 0)], ds[(0, 0, 1)]
    dd = ds[(1, 1, 0)] + ds[(1, -1, 0)]
    ee = ds[(1, 0, 1)] + ds[(1, 0, -1)]
    ff = ds[(0, 1, 1)] + ds[(0, 1, -1)]
    s1 = ax + ay + az
    s2 = dd + ee + ff
    p1 = 3.0 * ax - s1
    p2 = s2 - 3.0 * ff
    q1 = ay - az
    q2 = dd - ee
    t0 = rate(0) * (d0 + s1 + s2)
    t1 = rate(1) * (8.0 * s2 - 11.0 * s1 - 30.0 * d0)
    t2 = rate(2) * (12.0 * d0 - 4.0 * s1 + s2)
    t9 = rate(9) * (p1 + p2)
    t10 = rate(10) * (p2 - 2.0 * p1)
    t11 = rate(11) * (q1 + q2)
    t12 = rate(12) * (q2 - 2.0 * q1)
    t13 = rate(13) * (ds[(1, 1, 0)] - ds[(1, -1, 0)])
    t14 = rate(14) * (ds[(0, 1, 1)] - ds[(0, 1, -1)])
    t15 = rate(15) * (ds[(1, 0, 1)] - ds[(1, 0, -1)])
    base1 = t0 - 11.0 * t1 - 4.0 * t2
    base2 = t0 + 8.0 * t1 + t2
    u1 = t9 - 2.0 * t10
    v1 = t11 - 2.0 * t12
    u2 = t9 + t10
    v2 = t11 + t12
    xy, xz, yz = base2 + u2 + v2, base2 + u2 - v2, base2 - 2.0 * u2
    even = {
        (1, 0, 0): base1 + 2.0 * u1, (0, 1, 0): base1 - u1 + v1, (0, 0, 1): base1 - u1 - v1,
        (1, 1, 0): xy + t13, (1, -1, 0): xy - t13,
        (1, 0, 1): xz + t15, (1, 0, -1): xz - t15,
        (0, 1, 1): yz + t14, (0, 1, -1): yz - t14,
    }
    even0 = t0 - 30.0 * t1 + 12.0 * t2
    x1, x2, y1, y2, z1, z2 = odd_sums(da)
    xs, ys, zs = x1 + x2, y1 + y2, z1 + z2
    t3 = rate(3) * (da[(1, 0, 0)] + xs)
    t4 = rate(4) * (xs - 4.0 * da[(1, 0, 0)])
    t5 = rate(5) * (da[(0, 1, 0)] + ys)
    t6 = rate(6) * (ys - 4.0 * da[(0, 1, 0)])
    t7 = rate(7) * (da[(0, 0, 1)] + zs)
    t8 = rate(8) * (zs - 4.0 * da[(0, 0, 1)])
    t16 = rate(16) * (x1 - x2)
    t17 = rate(17) * (y2 - y1)
    t18 = rate(18) * (z1 - z2)
    px, py, pz = t3 + t4, t5 + t6, t7 + t8
    xa, xb = px + t16, px - t16
    ya, yb = py - t17, py + t17
    za, zb = pz + t18, pz - t18
    odd = {
        (1, 0, 0): t3 - 4.0 * t4, (0, 1, 0): t5 - 4.0 * t6, (0, 0, 1): t7 - 4.0 * t8,
        (1, 1, 0): xa + ya, (1, -1, 0): xa - ya,
        (1, 0, 1): xb + za, (1, 0, -1): xb - za,
        (0, 1, 1): yb + zb, (0, 1, -1): yb - zb,
    }
    fluid, wall, inlet = kind == 0, kind == 1, kind == 2
    speed = (0.0, 0.0, INLET_SPEED)
    still = 1.0 - 1.5 * INLET_SPEED**2
    out = [None] * 19
    out[0] = jnp.where(
        fluid, f[0] - even0,
        jnp.where(wall, f[0], jnp.where(inlet, WEIGHTS[0] * still, WEIGHTS[0] * outlet_base)),
    )
    for c in pos:
        dot = sum(p * v for p, v in zip(c, speed))
        half, lean = 0.5 * s[c], 0.5 * a[c]
        ev = jnp.where(
            inlet, weight[c] * (still + 4.5 * dot * dot), weight[c] * (outlet_base + quad[c])
        )
        od = jnp.where(inlet, 3.0 * weight[c] * dot, (3.0 * weight[c]) * cj[c])
        ev = jnp.where(fluid, half - even[c], jnp.where(wall, half, ev))
        od = jnp.where(fluid, lean - odd[c], jnp.where(wall, -lean, od))
        out[INDEX[c]] = ev + od
        out[19 - INDEX[c]] = ev - od
    return out


def kernel(
    n, held, cap, pop_hbm, rates, dest_s, dest_v, flags_v, links_v, out,
    near, low, high, flags_low, flags_high, links_low, links_high, dest_low,
    kinds, reach, hops, split, second, result, send, recv, own_sem,
):
    me = lax.axis_index("blk")
    has_low, has_high = me > 0, me < n - 1
    span_low, span_high = 3 * LAYER, 2 * LAYER
    rows = span_low + held + span_high
    inner = rows - 2 * LAYER
    final = held + LAYER

    barrier = pltpu.get_barrier_semaphore()

    @pl.when(has_high)
    def _():
        pl.semaphore_signal(barrier, inc=1, device_id=(me + 1,), device_id_type=MESH)

    @pl.when(has_low)
    def _():
        pl.semaphore_signal(barrier, inc=1, device_id=(me - 1,), device_id_type=MESH)

    own = pltpu.make_async_copy(pop_hbm, near, own_sem)
    own.start()

    def copy(i, src, dst, target):
        return pltpu.make_async_remote_copy(
            src_ref=src, dst_ref=dst, send_sem=send.at[i], recv_sem=recv.at[i],
            device_id=(target,), device_id_type=MESH,
        )

    up_meta = [
        copy(0, dest_v, dest_low, me + 1),
        copy(1, links_v, links_low, me + 1),
        copy(2, flags_v, flags_low, me + 1),
    ]
    down_meta = [
        copy(3, links_v, links_high, me - 1),
        copy(4, flags_v, flags_high, me - 1),
    ]
    up_pop = copy(5, pop_hbm.at[:, pl.ds(held - span_low, span_low)], low, me + 1)
    down_pop = copy(6, pop_hbm.at[:, pl.ds(0, span_high)], high, me - 1)
    ups, downs = up_meta + [up_pop], down_meta + [down_pop]

    @pl.when(has_low & has_high)
    def _():
        pl.semaphore_wait(barrier, 2)

    @pl.when(jnp.logical_not(has_low & has_high))
    def _():
        pl.semaphore_wait(barrier, 1)

    @pl.when(has_high)
    def _():
        for c in ups:
            c.start()

    @pl.when(has_low)
    def _():
        for c in downs:
            c.start()

    @pl.when(jnp.logical_not(has_low))
    def _():
        low[...] = jnp.zeros_like(low)
        flags_low[...] = jnp.zeros_like(flags_low)
        links_low[...] = jnp.zeros_like(links_low)
        dest_low[...] = jnp.zeros_like(dest_low)

    @pl.when(jnp.logical_not(has_high))
    def _():
        high[...] = jnp.zeros_like(high)
        flags_high[...] = jnp.zeros_like(flags_high)
        links_high[...] = jnp.zeros_like(links_high)

    scale = [rates[k] * (1.0 / NORMS[k]) for k in range(19)]

    def settle(load, kind_at, row, store):
        f = [load(q) for q in range(19)]
        g = collide(f, kind_at, lambda k: scale[k])
        for q in range(19):
            store(q, row, g[q])

    def keep(q, row, value):
        if q > 0:
            high_part = value.astype(jnp.bfloat16)
            low_part = (value - high_part.astype(jnp.float32)).astype(jnp.bfloat16)
            split[q - 1, pl.ds(row, CHUNK), 0:SITES] = high_part
            split[q - 1, pl.ds(row, CHUNK), SITES : 2 * SITES] = low_part

    @pl.when(has_low)
    def _():
        for c in up_meta:
            c.wait_recv()

    @pl.when(has_high)
    def _():
        for c in down_meta:
            c.wait_recv()

    came = dest_v[0:1, 0:1] - me * cap
    came_low = dest_low[0:1, 0:1] - (me - 1) * cap
    gone = jnp.sum(
        jnp.where(dest_v[...] >= (me + 1) * cap, 1.0, 0.0), axis=1, keepdims=True
    ).astype(jnp.int32)

    base_low = held * -1 + span_low - came_low
    base_own = span_low - came
    base_high = span_low + held - gone
    lane_slot = lax.broadcasted_iota(jnp.int32, (1, cap), 1)
    pos_low = base_low + lane_slot
    pos_own = base_own + lane_slot
    pos_high = base_high + lane_slot
    pos_low = jnp.where((pos_low < base_own) & has_low, pos_low, -1)
    pos_own = jnp.where(pos_own < base_high, pos_own, -1)
    pos_high = jnp.where(has_high, pos_high, -1)
    row_id = lax.broadcasted_iota(jnp.int32, (rows, cap), 0)
    picks = [
        jnp.where(row_id == p, 1.0, 0.0).astype(jnp.bfloat16) for p in (pos_low, pos_own, pos_high)
    ]
    total = None
    for pick, ref in zip(picks, (flags_low, flags_v, flags_high)):
        part = jnp.dot(
            pick, ref[...].astype(jnp.float32).astype(jnp.bfloat16),
            preferred_element_type=jnp.float32,
        )
        total = part if total is None else total + part
    kinds[...] = (total + 0.5).astype(jnp.int32)

    total = None
    for pick, ref in zip(picks, (links_low, links_v, links_high)):
        link = ref[...]
        where = jnp.where(
            link >= (me + 1) * cap, base_high + (link - (me + 1) * cap),
            jnp.where(link >= me * cap, base_own + (link - me * cap), base_low + (link - (me - 1) * cap)),
        )
        where = jnp.where((link >= 0) & (where >= 0) & (where < rows), where + 1, 0)
        part = lax.dot_general(
            pick[LAYER : LAYER + inner], where.astype(jnp.float32).astype(jnp.bfloat16),
            (((1,), (1,)), ((), ())), preferred_element_type=jnp.float32,
        )
        total = part if total is None else total + part
    reach[...] = total
    source_id = lax.broadcasted_iota(jnp.int32, (inner, rows), 1).astype(jnp.float32) + 1.0
    for d in range(18):
        column = jnp.broadcast_to(reach[:, d : d + 1], (inner, rows))
        hops[d] = jnp.where(column == source_id, 1.0, 0.0).astype(jnp.bfloat16)

    own.wait()

    def first(ref, base, count):
        def step(i, carry):
            at = pl.multiple_of(i * CHUNK, CHUNK)
            row = pl.multiple_of(base + at, CHUNK)

            def store(q, row, value):
                keep(q, row, value)
                ref[q, pl.ds(at, CHUNK), :] = value

            settle(lambda q: ref[q, pl.ds(at, CHUNK), :], kinds[pl.ds(row, CHUNK), :], row, store)
            return carry

        lax.fori_loop(0, count // CHUNK, step, 0)

    first(near, span_low, held)

    @pl.when(has_low)
    def _():
        up_pop.wait_recv()

    first(low, 0, span_low)

    @pl.when(has_high)
    def _():
        down_pop.wait_recv()

    first(high, span_low + held, span_high)

    def stream(q, own_q, own_opp, lo, count):
        lane = lax.broadcasted_iota(jnp.int32, (count, SITES), 1)
        cx, cy, cz = VELOCITIES[q]
        moved = rolled(own_q, 32 * cx + 8 * cy + cz)
        value = jnp.where(lane_region(q, (0, 0, 0), lane), moved, own_opp)
        entries = regions_of(q)
        picks = [hops[d, lo : lo + count, :] for d, _, _ in entries]
        pick = picks[0] if len(picks) == 1 else jnp.concatenate(picks, axis=0)
        got = jnp.dot(pick, split[q - 1], preferred_element_type=jnp.float32)
        got = got[:, 0:SITES] + got[:, SITES : 2 * SITES]
        for i, (d, step, shift) in enumerate(entries):
            present = jnp.broadcast_to(reach[lo : lo + count, d : d + 1], (count, SITES)) > 0.0
            use = jnp.logical_and(lane_region(q, step, lane), present)
            value = jnp.where(use, rolled(got[i * count : (i + 1) * count], shift), value)
        return value

    def whole(q):
        return jnp.concatenate(
            [low[q, LAYER:span_low, :], near[q], high[q, 0:LAYER, :]], axis=0
        )

    second[0] = whole(0)
    for q in range(1, 19):
        second[q] = stream(q, whole(q), whole(19 - q), 0, inner)

    def again(i, carry):
        at = pl.multiple_of(i * CHUNK, CHUNK)
        row = pl.multiple_of(at + LAYER, CHUNK)

        def store(q, row, value):
            keep(q, row, value)
            second[q, pl.ds(at, CHUNK), :] = value

        settle(lambda q: second[q, pl.ds(at, CHUNK), :], kinds[pl.ds(row, CHUNK), :], row, store)
        return carry

    lax.fori_loop(0, inner // CHUNK, again, 0)

    row_of = lax.broadcasted_iota(jnp.int32, (final, SITES), 0)
    full = row_of < final - gone
    skip = jnp.clip(LAYER - (dest_s[0] - me * cap), 0, LAYER)
    for q in range(19):
        if q == 0:
            value = second[0, LAYER : LAYER + final, :]
        else:
            value = stream(
                q, second[q, LAYER : LAYER + final, :], second[19 - q, LAYER : LAYER + final, :],
                LAYER, final,
            )
        result[q, 0:final, :] = jnp.where(full, value, 0.0)
        result[q, final : final + LAYER, :] = jnp.zeros((LAYER, SITES), jnp.float32)
        out[q] = result[q, pl.ds(skip, cap), :]

    @pl.when(has_high)
    def _():
        for c in ups:
            c.wait_send()

    @pl.when(has_low)
    def _():
        for c in downs:
            c.wait_send()


def local(populations, relax_rates, destination, block_links, site_flags):
    n = lax.axis_size("blk")
    held, cap = populations.shape[0], site_flags.shape[0]
    rows = held + 5 * LAYER
    inner, final = rows - 2 * LAYER, held + LAYER
    vmem = pl.BlockSpec(memory_space=pltpu.VMEM)
    smem = pl.BlockSpec(memory_space=pltpu.SMEM)
    f32, i32 = jnp.float32, jnp.int32
    out = pl.pallas_call(
        functools.partial(kernel, n, held, cap),
        out_shape=jax.ShapeDtypeStruct((Q, cap, SITES), f32),
        in_specs=[pl.BlockSpec(memory_space=pl.ANY), smem, smem, vmem, vmem, vmem],
        out_specs=vmem,
        scratch_shapes=[
            pltpu.VMEM((Q, held, SITES), f32),
            pltpu.VMEM((Q, 3 * LAYER, SITES), f32),
            pltpu.VMEM((Q, 2 * LAYER, SITES), f32),
            pltpu.VMEM((cap, SITES), i32),
            pltpu.VMEM((cap, SITES), i32),
            pltpu.VMEM((18, cap), i32),
            pltpu.VMEM((18, cap), i32),
            pltpu.VMEM((1, held), i32),
            pltpu.VMEM((rows, SITES), i32),
            pltpu.VMEM((inner, 18), f32),
            pltpu.VMEM((18, inner, rows), jnp.bfloat16),
            pltpu.VMEM((18, rows, 2 * SITES), jnp.bfloat16),
            pltpu.VMEM((Q, inner, SITES), f32),
            pltpu.VMEM((Q, final + LAYER, SITES), f32),
            pltpu.SemaphoreType.DMA((7,)),
            pltpu.SemaphoreType.DMA((7,)),
            pltpu.SemaphoreType.DMA,
        ],
        compiler_params=pltpu.CompilerParams(
            collective_id=0, has_side_effects=True, vmem_limit_bytes=48 * 1024 * 1024
        ),
    )(
        jnp.transpose(populations, (1, 0, 2)), relax_rates, destination,
        destination.reshape(1, held), site_flags, jnp.transpose(block_links, (1, 0)),
    )
    return jnp.transpose(out, (1, 0, 2))


def solution(mesh):
    in_specs = (P("blk", None, None), P(), P("blk"), P("blk", None), P("blk", None))
    out_specs = P("blk", None, None)
    return jax.shard_map(local, mesh=mesh, in_specs=in_specs, out_specs=out_specs, check_vma=False)
```

```python
import functools

import jax
import jax.numpy as jnp
import numpy as np
from jax import lax
from jax.experimental import pallas as pl
from jax.experimental.pallas import tpu as pltpu
from jax.sharding import PartitionSpec as P

Q = 19
SITES = 128
LAYER = 16
INLET_SPEED = 0.05
CHUNK = 16
MESH = pl.DeviceIdType.MESH

OFFSETS = [
    (x, y, z)
    for x in (-1, 0, 1)
    for y in (-1, 0, 1)
    for z in (-1, 0, 1)
    if 1 <= abs(x) + abs(y) + abs(z) <= 2
]
VELOCITIES = [(0, 0, 0)] + OFFSETS
WEIGHTS = [(1 / 3, 1 / 18, 1 / 36)[sum(abs(e) for e in c)] for c in VELOCITIES]
INDEX = {c: q for q, c in enumerate(VELOCITIES)}
PAIRS = [q for q in range(10, 19)]


def moment_norms():
    c = np.array(VELOCITIES, np.float64)
    x, y, z = c.T
    e = x * x + y * y + z * z
    f = 5 * e - 9
    s = 3 * e - 5
    xx = 3 * x * x - e
    ww = y * y - z * z
    rows = [
        np.ones(19), 19 * e - 30, (21 * e * e - 53 * e + 24) / 2, x, f * x, y, f * y, z, f * z,
        xx, s * xx, ww, s * ww, x * y, y * z, x * z,
        (y * y - z * z) * x, (z * z - x * x) * y, (x * x - y * y) * z,
    ]
    return [float(np.sum(r * r)) for r in rows]


NORMS = moment_norms()


def regions_of(q):
    cx, cy, cz = VELOCITIES[q]
    found = []
    for nx in sorted({0, -cx}):
        for ny in sorted({0, -cy}):
            for nz in sorted({0, -cz}):
                if (nx, ny, nz) == (0, 0, 0):
                    continue
                shift = (32 * cx + 8 * cy + cz + 32 * ny + 8 * nz) % SITES
                found.append((INDEX[(nx, ny, nz)] - 1, (nx, ny, nz), shift))
    return found


def lane_region(q, step, lane):
    cx, cy, cz = VELOCITIES[q]
    mask = None
    for c, n, value, side in (
        (cx, step[0], lane // 32, 4),
        (cy, step[1], (lane // 8) % 4, 4),
        (cz, step[2], lane % 8, 8),
    ):
        if c == 0:
            continue
        edge = 0 if c > 0 else side - 1
        part = (value == edge) if n != 0 else (value != edge)
        mask = part if mask is None else jnp.logical_and(mask, part)
    return mask


def rolled(value, shift):
    return value if shift % SITES == 0 else pltpu.roll(value, shift % SITES, 1)


def combos(get, jx, jy, jz):
    return {
        (0, 0, 1): jz, (0, 1, 0): jy, (1, 0, 0): jx,
        (0, 1, 1): jy + jz, (0, 1, -1): jy - jz,
        (1, 0, 1): jx + jz, (1, 0, -1): jx - jz,
        (1, 1, 0): jx + jy, (1, -1, 0): jx - jy,
    }


def odd_sums(a):
    x1 = a[(1, 1, 0)] + a[(1, -1, 0)]
    x2 = a[(1, 0, 1)] + a[(1, 0, -1)]
    y1 = a[(1, 1, 0)] - a[(1, -1, 0)]
    y2 = a[(0, 1, 1)] + a[(0, 1, -1)]
    z1 = a[(1, 0, 1)] - a[(1, 0, -1)]
    z2 = a[(0, 1, 1)] - a[(0, 1, -1)]
    return x1, x2, y1, y2, z1, z2


def collide(f, kind, rate):
    pos = [VELOCITIES[q] for q in PAIRS]
    weight = {c: WEIGHTS[INDEX[c]] for c in pos}
    s = {c: f[INDEX[c]] + f[19 - INDEX[c]] for c in pos}
    a = {c: f[INDEX[c]] - f[19 - INDEX[c]] for c in pos}
    density = f[0]
    for c in pos:
        density = density + s[c]
    x1, x2, y1, y2, z1, z2 = odd_sums(a)
    jx = a[(1, 0, 0)] + x1 + x2
    jy = a[(0, 1, 0)] + y1 + y2
    jz = a[(0, 0, 1)] + z1 + z2
    cj = combos(None, jx, jy, jz)
    square = 1.5 * (jx * jx + jy * jy + jz * jz)
    outlet_base = 1.0 - square
    fluid_base = density - square
    quad = {c: 4.5 * (cj[c] * cj[c]) for c in pos}
    d0 = f[0] - WEIGHTS[0] * fluid_base
    ds = {c: s[c] - (2 * weight[c]) * (fluid_base + quad[c]) for c in pos}
    da = {c: a[c] - (6 * weight[c]) * cj[c] for c in pos}
    ax, ay, az = ds[(1, 0, 0)], ds[(0, 1, 0)], ds[(0, 0, 1)]
    dd = ds[(1, 1, 0)] + ds[(1, -1, 0)]
    ee = ds[(1, 0, 1)] + ds[(1, 0, -1)]
    ff = ds[(0, 1, 1)] + ds[(0, 1, -1)]
    s1 = ax + ay + az
    s2 = dd + ee + ff
    p1 = 3.0 * ax - s1
    p2 = s2 - 3.0 * ff
    q1 = ay - az
    q2 = dd - ee
    t0 = rate(0) * (d0 + s1 + s2)
    t1 = rate(1) * (8.0 * s2 - 11.0 * s1 - 30.0 * d0)
    t2 = rate(2) * (12.0 * d0 - 4.0 * s1 + s2)
    t9 = rate(9) * (p1 + p2)
    t10 = rate(10) * (p2 - 2.0 * p1)
    t11 = rate(11) * (q1 + q2)
    t12 = rate(12) * (q2 - 2.0 * q1)
    t13 = rate(13) * (ds[(1, 1, 0)] - ds[(1, -1, 0)])
    t14 = rate(14) * (ds[(0, 1, 1)] - ds[(0, 1, -1)])
    t15 = rate(15) * (ds[(1, 0, 1)] - ds[(1, 0, -1)])
    base1 = t0 - 11.0 * t1 - 4.0 * t2
    base2 = t0 + 8.0 * t1 + t2
    u1 = t9 - 2.0 * t10
    v1 = t11 - 2.0 * t12
    u2 = t9 + t10
    v2 = t11 + t12
    xy, xz, yz = base2 + u2 + v2, base2 + u2 - v2, base2 - 2.0 * u2
    even = {
        (1, 0, 0): base1 + 2.0 * u1, (0, 1, 0): base1 - u1 + v1, (0, 0, 1): base1 - u1 - v1,
        (1, 1, 0): xy + t13, (1, -1, 0): xy - t13,
        (1, 0, 1): xz + t15, (1, 0, -1): xz - t15,
        (0, 1, 1): yz + t14, (0, 1, -1): yz - t14,
    }
    even0 = t0 - 30.0 * t1 + 12.0 * t2
    x1, x2, y1, y2, z1, z2 = odd_sums(da)
    xs, ys, zs = x1 + x2, y1 + y2, z1 + z2
    t3 = rate(3) * (da[(1, 0, 0)] + xs)
    t4 = rate(4) * (xs - 4.0 * da[(1, 0, 0)])
    t5 = rate(5) * (da[(0, 1, 0)] + ys)
    t6 = rate(6) * (ys - 4.0 * da[(0, 1, 0)])
    t7 = rate(7) * (da[(0, 0, 1)] + zs)
    t8 = rate(8) * (zs - 4.0 * da[(0, 0, 1)])
    t16 = rate(16) * (x1 - x2)
    t17 = rate(17) * (y2 - y1)
    t18 = rate(18) * (z1 - z2)
    px, py, pz = t3 + t4, t5 + t6, t7 + t8
    xa, xb = px + t16, px - t16
    ya, yb = py - t17, py + t17
    za, zb = pz + t18, pz - t18
    odd = {
        (1, 0, 0): t3 - 4.0 * t4, (0, 1, 0): t5 - 4.0 * t6, (0, 0, 1): t7 - 4.0 * t8,
        (1, 1, 0): xa + ya, (1, -1, 0): xa - ya,
        (1, 0, 1): xb + za, (1, 0, -1): xb - za,
        (0, 1, 1): yb + zb, (0, 1, -1): yb - zb,
    }
    fluid, wall, inlet = kind == 0, kind == 1, kind == 2
    speed = (0.0, 0.0, INLET_SPEED)
    still = 1.0 - 1.5 * INLET_SPEED**2
    out = [None] * 19
    out[0] = jnp.where(
        fluid, f[0] - even0,
        jnp.where(wall, f[0], jnp.where(inlet, WEIGHTS[0] * still, WEIGHTS[0] * outlet_base)),
    )
    for c in pos:
        dot = sum(p * v for p, v in zip(c, speed))
        half, lean = 0.5 * s[c], 0.5 * a[c]
        ev = jnp.where(
            inlet, weight[c] * (still + 4.5 * dot * dot), weight[c] * (outlet_base + quad[c])
        )
        od = jnp.where(inlet, 3.0 * weight[c] * dot, (3.0 * weight[c]) * cj[c])
        ev = jnp.where(fluid, half - even[c], jnp.where(wall, half, ev))
        od = jnp.where(fluid, lean - odd[c], jnp.where(wall, -lean, od))
        out[INDEX[c]] = ev + od
        out[19 - INDEX[c]] = ev - od
    return out


def kernel(
    n, held, cap, pop_hbm, rates_hbm, dest_hbm, flags_hbm, links_hbm, out,
    near, low, high, flags_low, flags_high, links_low, links_high, dest_low,
    kinds, reach, hops, split, second, result, rates, dest_s, dest_v, flags_v, links_v,
    send, recv, own_sem,
):
    me = lax.axis_index("blk")
    has_low, has_high = me > 0, me < n - 1
    span_low, span_high = 3 * LAYER, 2 * LAYER
    rows = span_low + held + span_high
    inner = rows - 2 * LAYER
    final = held + LAYER

    barrier = pltpu.get_barrier_semaphore()

    @pl.when(has_high)
    def _():
        pl.semaphore_signal(barrier, inc=1, device_id=(me + 1,), device_id_type=MESH)

    @pl.when(has_low)
    def _():
        pl.semaphore_signal(barrier, inc=1, device_id=(me - 1,), device_id_type=MESH)

    small = [
        pltpu.make_async_copy(src, dst, own_sem.at[i])
        for i, (src, dst) in enumerate((
            (rates_hbm, rates), (dest_hbm, dest_s), (dest_hbm, dest_v),
            (flags_hbm, flags_v), (links_hbm, links_v),
        ))
    ]
    for c in small:
        c.start()
    own = pltpu.make_async_copy(pop_hbm, near, own_sem.at[5])
    own.start()

    def copy(i, src, dst, target):
        return pltpu.make_async_remote_copy(
            src_ref=src, dst_ref=dst, send_sem=send.at[i], recv_sem=recv.at[i],
            device_id=(target,), device_id_type=MESH,
        )

    up_meta = [
        copy(0, dest_hbm, dest_low, me + 1),
        copy(1, links_hbm, links_low, me + 1),
        copy(2, flags_hbm, flags_low, me + 1),
    ]
    down_meta = [
        copy(3, links_hbm, links_high, me - 1),
        copy(4, flags_hbm, flags_high, me - 1),
    ]
    up_pop = copy(5, pop_hbm.at[:, pl.ds(held - span_low, span_low)], low, me + 1)
    down_pop = copy(6, pop_hbm.at[:, pl.ds(0, span_high)], high, me - 1)
    ups, downs = up_meta + [up_pop], down_meta + [down_pop]

    @pl.when(has_low & has_high)
    def _():
        pl.semaphore_wait(barrier, 2)

    @pl.when(jnp.logical_not(has_low & has_high))
    def _():
        pl.semaphore_wait(barrier, 1)

    @pl.when(has_high)
    def _():
        for c in ups:
            c.start()

    @pl.when(has_low)
    def _():
        for c in downs:
            c.start()

    @pl.when(jnp.logical_not(has_low))
    def _():
        low[...] = jnp.zeros_like(low)
        flags_low[...] = jnp.zeros_like(flags_low)
        links_low[...] = jnp.zeros_like(links_low)
        dest_low[...] = jnp.zeros_like(dest_low)

    @pl.when(jnp.logical_not(has_high))
    def _():
        high[...] = jnp.zeros_like(high)
        flags_high[...] = jnp.zeros_like(flags_high)
        links_high[...] = jnp.zeros_like(links_high)

    for c in small:
        c.wait()
    scale = [rates[0, k] * (1.0 / NORMS[k]) for k in range(19)]

    def settle(load, kind_at, row, store):
        f = [load(q) for q in range(19)]
        g = collide(f, kind_at, lambda k: scale[k])
        for q in range(19):
            store(q, row, g[q])

    def keep(q, row, value):
        if q > 0:
            high_part = value.astype(jnp.bfloat16)
            low_part = (value - high_part.astype(jnp.float32)).astype(jnp.bfloat16)
            split[q - 1, pl.ds(row, CHUNK), 0:SITES] = high_part
            split[q - 1, pl.ds(row, CHUNK), SITES : 2 * SITES] = low_part

    @pl.when(has_low)
    def _():
        for c in up_meta:
            c.wait_recv()

    @pl.when(has_high)
    def _():
        for c in down_meta:
            c.wait_recv()

    came = dest_v[0:1, 0:1] - me * cap
    came_low = dest_low[0:1, 0:1] - (me - 1) * cap
    gone = jnp.sum(
        jnp.where(dest_v[...] >= (me + 1) * cap, 1.0, 0.0), axis=1, keepdims=True
    ).astype(jnp.int32)

    base_low = held * -1 + span_low - came_low
    base_own = span_low - came
    base_high = span_low + held - gone
    lane_slot = lax.broadcasted_iota(jnp.int32, (1, cap), 1)
    pos_low = base_low + lane_slot
    pos_own = base_own + lane_slot
    pos_high = base_high + lane_slot
    pos_low = jnp.where((pos_low < base_own) & has_low, pos_low, -1)
    pos_own = jnp.where(pos_own < base_high, pos_own, -1)
    pos_high = jnp.where(has_high, pos_high, -1)
    row_id = lax.broadcasted_iota(jnp.int32, (rows, cap), 0)
    picks = [
        jnp.where(row_id == p, 1.0, 0.0).astype(jnp.bfloat16) for p in (pos_low, pos_own, pos_high)
    ]
    total = None
    for pick, ref in zip(picks, (flags_low, flags_v, flags_high)):
        part = jnp.dot(
            pick, ref[...].astype(jnp.float32).astype(jnp.bfloat16),
            preferred_element_type=jnp.float32,
        )
        total = part if total is None else total + part
    kinds[...] = (total + 0.5).astype(jnp.int32)

    total = None
    for pick, ref in zip(picks, (links_low, links_v, links_high)):
        link = ref[...]
        where = jnp.where(
            link >= (me + 1) * cap, base_high + (link - (me + 1) * cap),
            jnp.where(link >= me * cap, base_own + (link - me * cap), base_low + (link - (me - 1) * cap)),
        )
        where = jnp.where((link >= 0) & (where >= 0) & (where < rows), where + 1, 0)
        part = lax.dot_general(
            pick[LAYER : LAYER + inner], where.astype(jnp.float32).astype(jnp.bfloat16),
            (((1,), (1,)), ((), ())), preferred_element_type=jnp.float32,
        )
        total = part if total is None else total + part
    reach[...] = total
    source_id = lax.broadcasted_iota(jnp.int32, (inner, rows), 1).astype(jnp.float32) + 1.0
    for d in range(18):
        column = jnp.broadcast_to(reach[:, d : d + 1], (inner, rows))
        hops[d] = jnp.where(column == source_id, 1.0, 0.0).astype(jnp.bfloat16)

    own.wait()

    def first(ref, base, count):
        def step(i, carry):
            at = pl.multiple_of(i * CHUNK, CHUNK)
            row = pl.multiple_of(base + at, CHUNK)

            def store(q, row, value):
                keep(q, row, value)
                ref[q, pl.ds(at, CHUNK), :] = value

            settle(lambda q: ref[q, pl.ds(at, CHUNK), :], kinds[pl.ds(row, CHUNK), :], row, store)
            return carry

        lax.fori_loop(0, count // CHUNK, step, 0)

    first(near, span_low, held)

    @pl.when(has_low)
    def _():
        up_pop.wait_recv()

    first(low, 0, span_low)

    @pl.when(has_high)
    def _():
        down_pop.wait_recv()

    first(high, span_low + held, span_high)

    def stream(q, own_q, own_opp, lo, count):
        lane = lax.broadcasted_iota(jnp.int32, (count, SITES), 1)
        cx, cy, cz = VELOCITIES[q]
        moved = rolled(own_q, 32 * cx + 8 * cy + cz)
        value = jnp.where(lane_region(q, (0, 0, 0), lane), moved, own_opp)
        entries = regions_of(q)
        picks = [hops[d, lo : lo + count, :] for d, _, _ in entries]
        pick = picks[0] if len(picks) == 1 else jnp.concatenate(picks, axis=0)
        got = jnp.dot(pick, split[q - 1], preferred_element_type=jnp.float32)
        got = got[:, 0:SITES] + got[:, SITES : 2 * SITES]
        for i, (d, step, shift) in enumerate(entries):
            present = jnp.broadcast_to(reach[lo : lo + count, d : d + 1], (count, SITES)) > 0.0
            use = jnp.logical_and(lane_region(q, step, lane), present)
            value = jnp.where(use, rolled(got[i * count : (i + 1) * count], shift), value)
        return value

    def whole(q):
        return jnp.concatenate(
            [low[q, LAYER:span_low, :], near[q], high[q, 0:LAYER, :]], axis=0
        )

    second[0] = whole(0)
    for q in range(1, 19):
        second[q] = stream(q, whole(q), whole(19 - q), 0, inner)

    def again(i, carry):
        at = pl.multiple_of(i * CHUNK, CHUNK)
        row = pl.multiple_of(at + LAYER, CHUNK)

        def store(q, row, value):
            keep(q, row, value)
            second[q, pl.ds(at, CHUNK), :] = value

        settle(lambda q: second[q, pl.ds(at, CHUNK), :], kinds[pl.ds(row, CHUNK), :], row, store)
        return carry

    lax.fori_loop(0, inner // CHUNK, again, 0)

    row_of = lax.broadcasted_iota(jnp.int32, (final, SITES), 0)
    full = row_of < final - gone
    skip = jnp.clip(LAYER - (dest_s[0, 0] - me * cap), 0, LAYER)
    for q in range(19):
        if q == 0:
            value = second[0, LAYER : LAYER + final, :]
        else:
            value = stream(
                q, second[q, LAYER : LAYER + final, :], second[19 - q, LAYER : LAYER + final, :],
                LAYER, final,
            )
        result[q, 0:final, :] = jnp.where(full, value, 0.0)
        result[q, final : final + LAYER, :] = jnp.zeros((LAYER, SITES), jnp.float32)
        out[q] = result[q, pl.ds(skip, cap), :]

    @pl.when(has_high)
    def _():
        for c in ups:
            c.wait_send()

    @pl.when(has_low)
    def _():
        for c in downs:
            c.wait_send()


def local(populations, relax_rates, destination, block_links, site_flags):
    n = lax.axis_size("blk")
    held, cap = populations.shape[0], site_flags.shape[0]
    rows = held + 5 * LAYER
    inner, final = rows - 2 * LAYER, held + LAYER
    vmem = pl.BlockSpec(memory_space=pltpu.VMEM)
    f32, i32 = jnp.float32, jnp.int32
    out = pl.pallas_call(
        functools.partial(kernel, n, held, cap),
        out_shape=jax.ShapeDtypeStruct((Q, cap, SITES), f32),
        in_specs=[pl.BlockSpec(memory_space=pl.ANY)] * 5,
        out_specs=vmem,
        scratch_shapes=[
            pltpu.VMEM((Q, held, SITES), f32),
            pltpu.VMEM((Q, 3 * LAYER, SITES), f32),
            pltpu.VMEM((Q, 2 * LAYER, SITES), f32),
            pltpu.VMEM((cap, SITES), i32),
            pltpu.VMEM((cap, SITES), i32),
            pltpu.VMEM((18, cap), i32),
            pltpu.VMEM((18, cap), i32),
            pltpu.VMEM((1, held), i32),
            pltpu.VMEM((rows, SITES), i32),
            pltpu.VMEM((inner, 18), f32),
            pltpu.VMEM((18, inner, rows), jnp.bfloat16),
            pltpu.VMEM((18, rows, 2 * SITES), jnp.bfloat16),
            pltpu.VMEM((Q, inner, SITES), f32),
            pltpu.VMEM((Q, final + LAYER, SITES), f32),
            pltpu.SMEM((1, 19), f32),
            pltpu.SMEM((1, held), i32),
            pltpu.VMEM((1, held), i32),
            pltpu.VMEM((cap, SITES), i32),
            pltpu.VMEM((18, cap), i32),
            pltpu.SemaphoreType.DMA((7,)),
            pltpu.SemaphoreType.DMA((7,)),
            pltpu.SemaphoreType.DMA((6,)),
        ],
        compiler_params=pltpu.CompilerParams(
            collective_id=0, has_side_effects=True, vmem_limit_bytes=62 * 1024 * 1024
        ),
    )(
        jnp.transpose(populations, (1, 0, 2)), relax_rates.reshape(1, Q),
        destination.reshape(1, held), site_flags, jnp.transpose(block_links, (1, 0)),
    )
    return jnp.transpose(out, (1, 0, 2))


def solution(mesh):
    in_specs = (P("blk", None, None), P(), P("blk"), P("blk", None), P("blk", None))
    out_specs = P("blk", None, None)
    return jax.shard_map(local, mesh=mesh, in_specs=in_specs, out_specs=out_specs, check_vma=False)
```

```python
import functools

import jax
import jax.numpy as jnp
import numpy as np
from jax import lax
from jax.experimental import pallas as pl
from jax.experimental.pallas import tpu as pltpu
from jax.sharding import PartitionSpec as P

Q = 19
SITES = 128
LAYER = 16
INLET_SPEED = 0.05
CHUNK = 16
MESH = pl.DeviceIdType.MESH

OFFSETS = [
    (x, y, z)
    for x in (-1, 0, 1)
    for y in (-1, 0, 1)
    for z in (-1, 0, 1)
    if 1 <= abs(x) + abs(y) + abs(z) <= 2
]
VELOCITIES = [(0, 0, 0)] + OFFSETS
WEIGHTS = [(1 / 3, 1 / 18, 1 / 36)[sum(abs(e) for e in c)] for c in VELOCITIES]
INDEX = {c: q for q, c in enumerate(VELOCITIES)}
PAIRS = [q for q in range(10, 19)]


def moment_norms():
    c = np.array(VELOCITIES, np.float64)
    x, y, z = c.T
    e = x * x + y * y + z * z
    f = 5 * e - 9
    s = 3 * e - 5
    xx = 3 * x * x - e
    ww = y * y - z * z
    rows = [
        np.ones(19), 19 * e - 30, (21 * e * e - 53 * e + 24) / 2, x, f * x, y, f * y, z, f * z,
        xx, s * xx, ww, s * ww, x * y, y * z, x * z,
        (y * y - z * z) * x, (z * z - x * x) * y, (x * x - y * y) * z,
    ]
    return [float(np.sum(r * r)) for r in rows]


NORMS = moment_norms()


def regions_of(q):
    cx, cy, cz = VELOCITIES[q]
    found = []
    for nx in sorted({0, -cx}):
        for ny in sorted({0, -cy}):
            for nz in sorted({0, -cz}):
                if (nx, ny, nz) == (0, 0, 0):
                    continue
                shift = (32 * cx + 8 * cy + cz + 32 * ny + 8 * nz) % SITES
                found.append((INDEX[(nx, ny, nz)] - 1, (nx, ny, nz), shift))
    return found


def lane_region(q, step, lane):
    cx, cy, cz = VELOCITIES[q]
    mask = None
    for c, n, value, side in (
        (cx, step[0], lane // 32, 4),
        (cy, step[1], (lane // 8) % 4, 4),
        (cz, step[2], lane % 8, 8),
    ):
        if c == 0:
            continue
        edge = 0 if c > 0 else side - 1
        part = (value == edge) if n != 0 else (value != edge)
        mask = part if mask is None else jnp.logical_and(mask, part)
    return mask


def rolled(value, shift):
    return value if shift % SITES == 0 else pltpu.roll(value, shift % SITES, 1)


def combos(get, jx, jy, jz):
    return {
        (0, 0, 1): jz, (0, 1, 0): jy, (1, 0, 0): jx,
        (0, 1, 1): jy + jz, (0, 1, -1): jy - jz,
        (1, 0, 1): jx + jz, (1, 0, -1): jx - jz,
        (1, 1, 0): jx + jy, (1, -1, 0): jx - jy,
    }


def odd_sums(a):
    x1 = a[(1, 1, 0)] + a[(1, -1, 0)]
    x2 = a[(1, 0, 1)] + a[(1, 0, -1)]
    y1 = a[(1, 1, 0)] - a[(1, -1, 0)]
    y2 = a[(0, 1, 1)] + a[(0, 1, -1)]
    z1 = a[(1, 0, 1)] - a[(1, 0, -1)]
    z2 = a[(0, 1, 1)] - a[(0, 1, -1)]
    return x1, x2, y1, y2, z1, z2


def collide(f, kind, rate):
    pos = [VELOCITIES[q] for q in PAIRS]
    weight = {c: WEIGHTS[INDEX[c]] for c in pos}
    s = {c: f[INDEX[c]] + f[19 - INDEX[c]] for c in pos}
    a = {c: f[INDEX[c]] - f[19 - INDEX[c]] for c in pos}
    density = f[0]
    for c in pos:
        density = density + s[c]
    x1, x2, y1, y2, z1, z2 = odd_sums(a)
    jx = a[(1, 0, 0)] + x1 + x2
    jy = a[(0, 1, 0)] + y1 + y2
    jz = a[(0, 0, 1)] + z1 + z2
    cj = combos(None, jx, jy, jz)
    square = 1.5 * (jx * jx + jy * jy + jz * jz)
    outlet_base = 1.0 - square
    fluid_base = density - square
    quad = {c: 4.5 * (cj[c] * cj[c]) for c in pos}
    d0 = f[0] - WEIGHTS[0] * fluid_base
    ds = {c: s[c] - (2 * weight[c]) * (fluid_base + quad[c]) for c in pos}
    da = {c: a[c] - (6 * weight[c]) * cj[c] for c in pos}
    ax, ay, az = ds[(1, 0, 0)], ds[(0, 1, 0)], ds[(0, 0, 1)]
    dd = ds[(1, 1, 0)] + ds[(1, -1, 0)]
    ee = ds[(1, 0, 1)] + ds[(1, 0, -1)]
    ff = ds[(0, 1, 1)] + ds[(0, 1, -1)]
    s1 = ax + ay + az
    s2 = dd + ee + ff
    p1 = 3.0 * ax - s1
    p2 = s2 - 3.0 * ff
    q1 = ay - az
    q2 = dd - ee
    t0 = rate(0) * (d0 + s1 + s2)
    t1 = rate(1) * (8.0 * s2 - 11.0 * s1 - 30.0 * d0)
    t2 = rate(2) * (12.0 * d0 - 4.0 * s1 + s2)
    t9 = rate(9) * (p1 + p2)
    t10 = rate(10) * (p2 - 2.0 * p1)
    t11 = rate(11) * (q1 + q2)
    t12 = rate(12) * (q2 - 2.0 * q1)
    t13 = rate(13) * (ds[(1, 1, 0)] - ds[(1, -1, 0)])
    t14 = rate(14) * (ds[(0, 1, 1)] - ds[(0, 1, -1)])
    t15 = rate(15) * (ds[(1, 0, 1)] - ds[(1, 0, -1)])
    base1 = t0 - 11.0 * t1 - 4.0 * t2
    base2 = t0 + 8.0 * t1 + t2
    u1 = t9 - 2.0 * t10
    v1 = t11 - 2.0 * t12
    u2 = t9 + t10
    v2 = t11 + t12
    xy, xz, yz = base2 + u2 + v2, base2 + u2 - v2, base2 - 2.0 * u2
    even = {
        (1, 0, 0): base1 + 2.0 * u1, (0, 1, 0): base1 - u1 + v1, (0, 0, 1): base1 - u1 - v1,
        (1, 1, 0): xy + t13, (1, -1, 0): xy - t13,
        (1, 0, 1): xz + t15, (1, 0, -1): xz - t15,
        (0, 1, 1): yz + t14, (0, 1, -1): yz - t14,
    }
    even0 = t0 - 30.0 * t1 + 12.0 * t2
    x1, x2, y1, y2, z1, z2 = odd_sums(da)
    xs, ys, zs = x1 + x2, y1 + y2, z1 + z2
    t3 = rate(3) * (da[(1, 0, 0)] + xs)
    t4 = rate(4) * (xs - 4.0 * da[(1, 0, 0)])
    t5 = rate(5) * (da[(0, 1, 0)] + ys)
    t6 = rate(6) * (ys - 4.0 * da[(0, 1, 0)])
    t7 = rate(7) * (da[(0, 0, 1)] + zs)
    t8 = rate(8) * (zs - 4.0 * da[(0, 0, 1)])
    t16 = rate(16) * (x1 - x2)
    t17 = rate(17) * (y2 - y1)
    t18 = rate(18) * (z1 - z2)
    px, py, pz = t3 + t4, t5 + t6, t7 + t8
    xa, xb = px + t16, px - t16
    ya, yb = py - t17, py + t17
    za, zb = pz + t18, pz - t18
    odd = {
        (1, 0, 0): t3 - 4.0 * t4, (0, 1, 0): t5 - 4.0 * t6, (0, 0, 1): t7 - 4.0 * t8,
        (1, 1, 0): xa + ya, (1, -1, 0): xa - ya,
        (1, 0, 1): xb + za, (1, 0, -1): xb - za,
        (0, 1, 1): yb + zb, (0, 1, -1): yb - zb,
    }
    fluid, wall, inlet = kind == 0, kind == 1, kind == 2
    speed = (0.0, 0.0, INLET_SPEED)
    still = 1.0 - 1.5 * INLET_SPEED**2
    out = [None] * 19
    out[0] = jnp.where(
        fluid, f[0] - even0,
        jnp.where(wall, f[0], jnp.where(inlet, WEIGHTS[0] * still, WEIGHTS[0] * outlet_base)),
    )
    for c in pos:
        dot = sum(p * v for p, v in zip(c, speed))
        half, lean = 0.5 * s[c], 0.5 * a[c]
        ev = jnp.where(
            inlet, weight[c] * (still + 4.5 * dot * dot), weight[c] * (outlet_base + quad[c])
        )
        od = jnp.where(inlet, 3.0 * weight[c] * dot, (3.0 * weight[c]) * cj[c])
        ev = jnp.where(fluid, half - even[c], jnp.where(wall, half, ev))
        od = jnp.where(fluid, lean - odd[c], jnp.where(wall, -lean, od))
        out[INDEX[c]] = ev + od
        out[19 - INDEX[c]] = ev - od
    return out


def kernel(
    n, held, cap, pop_hbm, rates_hbm, dest_hbm, flags_hbm, links_hbm, out,
    near, low, high, flags_low, flags_high, links_low, links_high, dest_low,
    kinds, reach, hops, split, second, result, rates, dest_s, dest_v, flags_v, links_v,
    staged, send, recv, own_sem, out_sem,
):
    me = lax.axis_index("blk")
    has_low, has_high = me > 0, me < n - 1
    span_low, span_high = 3 * LAYER, 2 * LAYER
    rows = span_low + held + span_high
    inner = rows - 2 * LAYER
    final = held + LAYER

    barrier = pltpu.get_barrier_semaphore()

    @pl.when(has_high)
    def _():
        pl.semaphore_signal(barrier, inc=1, device_id=(me + 1,), device_id_type=MESH)

    @pl.when(has_low)
    def _():
        pl.semaphore_signal(barrier, inc=1, device_id=(me - 1,), device_id_type=MESH)

    small = [
        pltpu.make_async_copy(src, dst, own_sem.at[i])
        for i, (src, dst) in enumerate((
            (rates_hbm, rates), (dest_hbm, dest_s), (dest_hbm, dest_v),
            (flags_hbm, flags_v), (links_hbm, links_v),
        ))
    ]
    for c in small:
        c.start()
    own = pltpu.make_async_copy(pop_hbm, near, own_sem.at[5])
    own.start()

    def copy(i, src, dst, target):
        return pltpu.make_async_remote_copy(
            src_ref=src, dst_ref=dst, send_sem=send.at[i], recv_sem=recv.at[i],
            device_id=(target,), device_id_type=MESH,
        )

    up_meta = [
        copy(0, dest_hbm, dest_low, me + 1),
        copy(1, links_hbm, links_low, me + 1),
        copy(2, flags_hbm, flags_low, me + 1),
    ]
    down_meta = [
        copy(3, links_hbm, links_high, me - 1),
        copy(4, flags_hbm, flags_high, me - 1),
    ]
    up_pop = [
        copy(
            5 + i, pop_hbm.at[:, pl.ds(held - span_low + i * CHUNK, CHUNK)],
            low.at[:, pl.ds(i * CHUNK, CHUNK)], me + 1,
        )
        for i in range(span_low // CHUNK)
    ]
    down_pop = [
        copy(
            8 + i, pop_hbm.at[:, pl.ds(i * CHUNK, CHUNK)],
            high.at[:, pl.ds(i * CHUNK, CHUNK)], me - 1,
        )
        for i in range(span_high // CHUNK)
    ]
    ups, downs = up_meta + up_pop, down_meta + down_pop

    @pl.when(has_low & has_high)
    def _():
        pl.semaphore_wait(barrier, 2)

    @pl.when(jnp.logical_not(has_low & has_high))
    def _():
        pl.semaphore_wait(barrier, 1)

    @pl.when(has_high)
    def _():
        for c in ups:
            c.start()

    @pl.when(has_low)
    def _():
        for c in downs:
            c.start()

    @pl.when(jnp.logical_not(has_low))
    def _():
        low[...] = jnp.zeros_like(low)
        flags_low[...] = jnp.zeros_like(flags_low)
        links_low[...] = jnp.zeros_like(links_low)
        dest_low[...] = jnp.zeros_like(dest_low)

    @pl.when(jnp.logical_not(has_high))
    def _():
        high[...] = jnp.zeros_like(high)
        flags_high[...] = jnp.zeros_like(flags_high)
        links_high[...] = jnp.zeros_like(links_high)

    for c in small:
        c.wait()
    scale = [rates[0, k] * (1.0 / NORMS[k]) for k in range(19)]

    def settle(load, kind_at, row, store):
        f = [load(q) for q in range(19)]
        g = collide(f, kind_at, lambda k: scale[k])
        for q in range(19):
            store(q, row, g[q])

    def keep(q, row, value):
        if q > 0:
            high_part = value.astype(jnp.bfloat16)
            low_part = (value - high_part.astype(jnp.float32)).astype(jnp.bfloat16)
            split[q - 1, pl.ds(row, CHUNK), 0:SITES] = high_part
            split[q - 1, pl.ds(row, CHUNK), SITES : 2 * SITES] = low_part

    @pl.when(has_low)
    def _():
        for c in up_meta:
            c.wait_recv()

    @pl.when(has_high)
    def _():
        for c in down_meta:
            c.wait_recv()

    came = dest_v[0:1, 0:1] - me * cap
    came_low = dest_low[0:1, 0:1] - (me - 1) * cap
    gone = jnp.sum(
        jnp.where(dest_v[...] >= (me + 1) * cap, 1.0, 0.0), axis=1, keepdims=True
    ).astype(jnp.int32)

    base_low = held * -1 + span_low - came_low
    base_own = span_low - came
    base_high = span_low + held - gone
    lane_slot = lax.broadcasted_iota(jnp.int32, (1, cap), 1)
    pos_low = base_low + lane_slot
    pos_own = base_own + lane_slot
    pos_high = base_high + lane_slot
    pos_low = jnp.where((pos_low < base_own) & has_low, pos_low, -1)
    pos_own = jnp.where(pos_own < base_high, pos_own, -1)
    pos_high = jnp.where(has_high, pos_high, -1)
    row_id = lax.broadcasted_iota(jnp.int32, (rows, cap), 0)
    picks = [
        jnp.where(row_id == p, 1.0, 0.0).astype(jnp.bfloat16) for p in (pos_low, pos_own, pos_high)
    ]
    total = None
    for pick, ref in zip(picks, (flags_low, flags_v, flags_high)):
        part = jnp.dot(
            pick, ref[...].astype(jnp.float32).astype(jnp.bfloat16),
            preferred_element_type=jnp.float32,
        )
        total = part if total is None else total + part
    kinds[...] = (total + 0.5).astype(jnp.int32)

    total = None
    for pick, ref in zip(picks, (links_low, links_v, links_high)):
        link = ref[...]
        where = jnp.where(
            link >= (me + 1) * cap, base_high + (link - (me + 1) * cap),
            jnp.where(link >= me * cap, base_own + (link - me * cap), base_low + (link - (me - 1) * cap)),
        )
        where = jnp.where((link >= 0) & (where >= 0) & (where < rows), where + 1, 0)
        part = lax.dot_general(
            pick[LAYER : LAYER + inner], where.astype(jnp.float32).astype(jnp.bfloat16),
            (((1,), (1,)), ((), ())), preferred_element_type=jnp.float32,
        )
        total = part if total is None else total + part
    reach[...] = total
    source_id = lax.broadcasted_iota(jnp.int32, (inner, rows), 1).astype(jnp.float32) + 1.0
    for d in range(18):
        column = jnp.broadcast_to(reach[:, d : d + 1], (inner, rows))
        hops[d] = jnp.where(column == source_id, 1.0, 0.0).astype(jnp.bfloat16)

    own.wait()

    def first(ref, base, start, count):
        def step(i, carry):
            at = pl.multiple_of(start + i * CHUNK, CHUNK)
            row = pl.multiple_of(base + at, CHUNK)

            def store(q, row, value):
                keep(q, row, value)
                ref[q, pl.ds(at, CHUNK), :] = value

            settle(lambda q: ref[q, pl.ds(at, CHUNK), :], kinds[pl.ds(row, CHUNK), :], row, store)
            return carry

        lax.fori_loop(0, count // CHUNK, step, 0)

    first(near, span_low, 0, held)

    def arrive_low(i):
        @pl.when(has_low)
        def _():
            up_pop[i].wait_recv()

        first(low, 0, i * CHUNK, CHUNK)

    def arrive_high(i):
        @pl.when(has_high)
        def _():
            down_pop[i].wait_recv()

        first(high, span_low + held, i * CHUNK, CHUNK)

    arrive_low(0)
    arrive_high(0)
    arrive_low(1)
    arrive_high(1)
    arrive_low(2)

    def stream(q, own_q, own_opp, lo, count):
        lane = lax.broadcasted_iota(jnp.int32, (count, SITES), 1)
        cx, cy, cz = VELOCITIES[q]
        moved = rolled(own_q, 32 * cx + 8 * cy + cz)
        value = jnp.where(lane_region(q, (0, 0, 0), lane), moved, own_opp)
        entries = regions_of(q)
        picks = [hops[d, lo : lo + count, :] for d, _, _ in entries]
        pick = picks[0] if len(picks) == 1 else jnp.concatenate(picks, axis=0)
        got = jnp.dot(pick, split[q - 1], preferred_element_type=jnp.float32)
        got = got[:, 0:SITES] + got[:, SITES : 2 * SITES]
        for i, (d, step, shift) in enumerate(entries):
            present = jnp.broadcast_to(reach[lo : lo + count, d : d + 1], (count, SITES)) > 0.0
            use = jnp.logical_and(lane_region(q, step, lane), present)
            value = jnp.where(use, rolled(got[i * count : (i + 1) * count], shift), value)
        return value

    def whole(q):
        return jnp.concatenate(
            [low[q, LAYER:span_low, :], near[q], high[q, 0:LAYER, :]], axis=0
        )

    second[0] = whole(0)
    for q in range(1, 19):
        second[q] = stream(q, whole(q), whole(19 - q), 0, inner)

    def again(i, carry):
        at = pl.multiple_of(i * CHUNK, CHUNK)
        row = pl.multiple_of(at + LAYER, CHUNK)

        def store(q, row, value):
            keep(q, row, value)
            second[q, pl.ds(at, CHUNK), :] = value

        settle(lambda q: second[q, pl.ds(at, CHUNK), :], kinds[pl.ds(row, CHUNK), :], row, store)
        return carry

    lax.fori_loop(0, inner // CHUNK, again, 0)

    row_of = lax.broadcasted_iota(jnp.int32, (final, SITES), 0)
    full = row_of < final - gone
    skip = jnp.clip(LAYER - (dest_s[0, 0] - me * cap), 0, LAYER)
    leaving = []
    for q in range(19):
        if q == 0:
            value = second[0, LAYER : LAYER + final, :]
        else:
            value = stream(
                q, second[q, LAYER : LAYER + final, :], second[19 - q, LAYER : LAYER + final, :],
                LAYER, final,
            )
        result[q, 0:final, :] = jnp.where(full, value, 0.0)
        result[q, final : final + LAYER, :] = jnp.zeros((LAYER, SITES), jnp.float32)
        staged[q] = result[q, pl.ds(skip, cap), :]
        leave = pltpu.make_async_copy(staged.at[q], out.at[q], out_sem.at[q])
        leave.start()
        leaving.append(leave)

    for c in leaving:
        c.wait()

    @pl.when(has_high)
    def _():
        for c in ups:
            c.wait_send()

    @pl.when(has_low)
    def _():
        for c in downs:
            c.wait_send()


def local(populations, relax_rates, destination, block_links, site_flags):
    n = lax.axis_size("blk")
    held, cap = populations.shape[0], site_flags.shape[0]
    rows = held + 5 * LAYER
    inner, final = rows - 2 * LAYER, held + LAYER
    f32, i32 = jnp.float32, jnp.int32
    out = pl.pallas_call(
        functools.partial(kernel, n, held, cap),
        out_shape=jax.ShapeDtypeStruct((Q, cap, SITES), f32),
        in_specs=[pl.BlockSpec(memory_space=pl.ANY)] * 5,
        out_specs=pl.BlockSpec(memory_space=pl.ANY),
        scratch_shapes=[
            pltpu.VMEM((Q, held, SITES), f32),
            pltpu.VMEM((Q, 3 * LAYER, SITES), f32),
            pltpu.VMEM((Q, 2 * LAYER, SITES), f32),
            pltpu.VMEM((cap, SITES), i32),
            pltpu.VMEM((cap, SITES), i32),
            pltpu.VMEM((18, cap), i32),
            pltpu.VMEM((18, cap), i32),
            pltpu.VMEM((1, held), i32),
            pltpu.VMEM((rows, SITES), i32),
            pltpu.VMEM((inner, 18), f32),
            pltpu.VMEM((18, inner, rows), jnp.bfloat16),
            pltpu.VMEM((18, rows, 2 * SITES), jnp.bfloat16),
            pltpu.VMEM((Q, inner, SITES), f32),
            pltpu.VMEM((Q, final + LAYER, SITES), f32),
            pltpu.SMEM((1, 19), f32),
            pltpu.SMEM((1, held), i32),
            pltpu.VMEM((1, held), i32),
            pltpu.VMEM((cap, SITES), i32),
            pltpu.VMEM((18, cap), i32),
            pltpu.VMEM((Q, cap, SITES), f32),
            pltpu.SemaphoreType.DMA((10,)),
            pltpu.SemaphoreType.DMA((10,)),
            pltpu.SemaphoreType.DMA((6,)),
            pltpu.SemaphoreType.DMA((Q,)),
        ],
        compiler_params=pltpu.CompilerParams(
            collective_id=0, has_side_effects=True, vmem_limit_bytes=62 * 1024 * 1024
        ),
    )(
        jnp.transpose(populations, (1, 0, 2)), relax_rates.reshape(1, Q),
        destination.reshape(1, held), site_flags, jnp.transpose(block_links, (1, 0)),
    )
    return jnp.transpose(out, (1, 0, 2))


def solution(mesh):
    in_specs = (P("blk", None, None), P(), P("blk"), P("blk", None), P("blk", None))
    out_specs = P("blk", None, None)
    return jax.shard_map(local, mesh=mesh, in_specs=in_specs, out_specs=out_specs, check_vma=False)
```

```python
import functools

import jax
import jax.numpy as jnp
import numpy as np
from jax import lax
from jax.experimental import pallas as pl
from jax.experimental.pallas import tpu as pltpu
from jax.sharding import PartitionSpec as P

Q = 19
SITES = 128
LAYER = 16
INLET_SPEED = 0.05
CHUNK = 16
MESH = pl.DeviceIdType.MESH

OFFSETS = [
    (x, y, z)
    for x in (-1, 0, 1)
    for y in (-1, 0, 1)
    for z in (-1, 0, 1)
    if 1 <= abs(x) + abs(y) + abs(z) <= 2
]
VELOCITIES = [(0, 0, 0)] + OFFSETS
WEIGHTS = [(1 / 3, 1 / 18, 1 / 36)[sum(abs(e) for e in c)] for c in VELOCITIES]
INDEX = {c: q for q, c in enumerate(VELOCITIES)}
PAIRS = [q for q in range(10, 19)]


def moment_norms():
    c = np.array(VELOCITIES, np.float64)
    x, y, z = c.T
    e = x * x + y * y + z * z
    f = 5 * e - 9
    s = 3 * e - 5
    xx = 3 * x * x - e
    ww = y * y - z * z
    rows = [
        np.ones(19), 19 * e - 30, (21 * e * e - 53 * e + 24) / 2, x, f * x, y, f * y, z, f * z,
        xx, s * xx, ww, s * ww, x * y, y * z, x * z,
        (y * y - z * z) * x, (z * z - x * x) * y, (x * x - y * y) * z,
    ]
    return [float(np.sum(r * r)) for r in rows]


NORMS = moment_norms()


def regions_of(q):
    cx, cy, cz = VELOCITIES[q]
    found = []
    for nx in sorted({0, -cx}):
        for ny in sorted({0, -cy}):
            for nz in sorted({0, -cz}):
                if (nx, ny, nz) == (0, 0, 0):
                    continue
                shift = (32 * cx + 8 * cy + cz + 32 * ny + 8 * nz) % SITES
                found.append((INDEX[(nx, ny, nz)] - 1, (nx, ny, nz), shift))
    return found


def lane_region(q, step, lane):
    cx, cy, cz = VELOCITIES[q]
    mask = None
    for c, n, value, side in (
        (cx, step[0], lane // 32, 4),
        (cy, step[1], (lane // 8) % 4, 4),
        (cz, step[2], lane % 8, 8),
    ):
        if c == 0:
            continue
        edge = 0 if c > 0 else side - 1
        part = (value == edge) if n != 0 else (value != edge)
        mask = part if mask is None else jnp.logical_and(mask, part)
    return mask


def rolled(value, shift):
    return value if shift % SITES == 0 else pltpu.roll(value, shift % SITES, 1)


def combos(get, jx, jy, jz):
    return {
        (0, 0, 1): jz, (0, 1, 0): jy, (1, 0, 0): jx,
        (0, 1, 1): jy + jz, (0, 1, -1): jy - jz,
        (1, 0, 1): jx + jz, (1, 0, -1): jx - jz,
        (1, 1, 0): jx + jy, (1, -1, 0): jx - jy,
    }


def odd_sums(a):
    x1 = a[(1, 1, 0)] + a[(1, -1, 0)]
    x2 = a[(1, 0, 1)] + a[(1, 0, -1)]
    y1 = a[(1, 1, 0)] - a[(1, -1, 0)]
    y2 = a[(0, 1, 1)] + a[(0, 1, -1)]
    z1 = a[(1, 0, 1)] - a[(1, 0, -1)]
    z2 = a[(0, 1, 1)] - a[(0, 1, -1)]
    return x1, x2, y1, y2, z1, z2


def collide(f, kind, rate):
    pos = [VELOCITIES[q] for q in PAIRS]
    weight = {c: WEIGHTS[INDEX[c]] for c in pos}
    s = {c: f[INDEX[c]] + f[19 - INDEX[c]] for c in pos}
    a = {c: f[INDEX[c]] - f[19 - INDEX[c]] for c in pos}
    density = f[0]
    for c in pos:
        density = density + s[c]
    x1, x2, y1, y2, z1, z2 = odd_sums(a)
    jx = a[(1, 0, 0)] + x1 + x2
    jy = a[(0, 1, 0)] + y1 + y2
    jz = a[(0, 0, 1)] + z1 + z2
    cj = combos(None, jx, jy, jz)
    square = 1.5 * (jx * jx + jy * jy + jz * jz)
    outlet_base = 1.0 - square
    fluid_base = density - square
    quad = {c: 4.5 * (cj[c] * cj[c]) for c in pos}
    d0 = f[0] - WEIGHTS[0] * fluid_base
    ds = {c: s[c] - (2 * weight[c]) * (fluid_base + quad[c]) for c in pos}
    da = {c: a[c] - (6 * weight[c]) * cj[c] for c in pos}
    ax, ay, az = ds[(1, 0, 0)], ds[(0, 1, 0)], ds[(0, 0, 1)]
    dd = ds[(1, 1, 0)] + ds[(1, -1, 0)]
    ee = ds[(1, 0, 1)] + ds[(1, 0, -1)]
    ff = ds[(0, 1, 1)] + ds[(0, 1, -1)]
    s1 = ax + ay + az
    s2 = dd + ee + ff
    p1 = 3.0 * ax - s1
    p2 = s2 - 3.0 * ff
    q1 = ay - az
    q2 = dd - ee
    t0 = rate(0) * (d0 + s1 + s2)
    t1 = rate(1) * (8.0 * s2 - 11.0 * s1 - 30.0 * d0)
    t2 = rate(2) * (12.0 * d0 - 4.0 * s1 + s2)
    t9 = rate(9) * (p1 + p2)
    t10 = rate(10) * (p2 - 2.0 * p1)
    t11 = rate(11) * (q1 + q2)
    t12 = rate(12) * (q2 - 2.0 * q1)
    t13 = rate(13) * (ds[(1, 1, 0)] - ds[(1, -1, 0)])
    t14 = rate(14) * (ds[(0, 1, 1)] - ds[(0, 1, -1)])
    t15 = rate(15) * (ds[(1, 0, 1)] - ds[(1, 0, -1)])
    base1 = t0 - 11.0 * t1 - 4.0 * t2
    base2 = t0 + 8.0 * t1 + t2
    u1 = t9 - 2.0 * t10
    v1 = t11 - 2.0 * t12
    u2 = t9 + t10
    v2 = t11 + t12
    xy, xz, yz = base2 + u2 + v2, base2 + u2 - v2, base2 - 2.0 * u2
    even = {
        (1, 0, 0): base1 + 2.0 * u1, (0, 1, 0): base1 - u1 + v1, (0, 0, 1): base1 - u1 - v1,
        (1, 1, 0): xy + t13, (1, -1, 0): xy - t13,
        (1, 0, 1): xz + t15, (1, 0, -1): xz - t15,
        (0, 1, 1): yz + t14, (0, 1, -1): yz - t14,
    }
    even0 = t0 - 30.0 * t1 + 12.0 * t2
    x1, x2, y1, y2, z1, z2 = odd_sums(da)
    xs, ys, zs = x1 + x2, y1 + y2, z1 + z2
    t3 = rate(3) * (da[(1, 0, 0)] + xs)
    t4 = rate(4) * (xs - 4.0 * da[(1, 0, 0)])
    t5 = rate(5) * (da[(0, 1, 0)] + ys)
    t6 = rate(6) * (ys - 4.0 * da[(0, 1, 0)])
    t7 = rate(7) * (da[(0, 0, 1)] + zs)
    t8 = rate(8) * (zs - 4.0 * da[(0, 0, 1)])
    t16 = rate(16) * (x1 - x2)
    t17 = rate(17) * (y2 - y1)
    t18 = rate(18) * (z1 - z2)
    px, py, pz = t3 + t4, t5 + t6, t7 + t8
    xa, xb = px + t16, px - t16
    ya, yb = py - t17, py + t17
    za, zb = pz + t18, pz - t18
    odd = {
        (1, 0, 0): t3 - 4.0 * t4, (0, 1, 0): t5 - 4.0 * t6, (0, 0, 1): t7 - 4.0 * t8,
        (1, 1, 0): xa + ya, (1, -1, 0): xa - ya,
        (1, 0, 1): xb + za, (1, 0, -1): xb - za,
        (0, 1, 1): yb + zb, (0, 1, -1): yb - zb,
    }
    fluid, wall, inlet = kind == 0, kind == 1, kind == 2
    speed = (0.0, 0.0, INLET_SPEED)
    still = 1.0 - 1.5 * INLET_SPEED**2
    out = [None] * 19
    out[0] = jnp.where(
        fluid, f[0] - even0,
        jnp.where(wall, f[0], jnp.where(inlet, WEIGHTS[0] * still, WEIGHTS[0] * outlet_base)),
    )
    for c in pos:
        dot = sum(p * v for p, v in zip(c, speed))
        half, lean = 0.5 * s[c], 0.5 * a[c]
        ev = jnp.where(
            inlet, weight[c] * (still + 4.5 * dot * dot), weight[c] * (outlet_base + quad[c])
        )
        od = jnp.where(inlet, 3.0 * weight[c] * dot, (3.0 * weight[c]) * cj[c])
        ev = jnp.where(fluid, half - even[c], jnp.where(wall, half, ev))
        od = jnp.where(fluid, lean - odd[c], jnp.where(wall, -lean, od))
        out[INDEX[c]] = ev + od
        out[19 - INDEX[c]] = ev - od
    return out


def kernel(
    n, held, cap, pop_hbm, rates_hbm, dest_hbm, flags_hbm, links_hbm, out,
    near, low, high, flags_low, flags_high, links_low, links_high, dest_low,
    kinds, reach, hops, split, second, result, rates, dest_s, dest_v, flags_v, links_v,
    send, recv, own_sem,
):
    me = lax.axis_index("blk")
    has_low, has_high = me > 0, me < n - 1
    span_low, span_high = 3 * LAYER, 2 * LAYER
    rows = span_low + held + span_high
    inner = rows - 2 * LAYER
    final = held + LAYER

    barrier = pltpu.get_barrier_semaphore()

    @pl.when(has_high)
    def _():
        pl.semaphore_signal(barrier, inc=1, device_id=(me + 1,), device_id_type=MESH)

    @pl.when(has_low)
    def _():
        pl.semaphore_signal(barrier, inc=1, device_id=(me - 1,), device_id_type=MESH)

    small = [
        pltpu.make_async_copy(src, dst, own_sem.at[i])
        for i, (src, dst) in enumerate((
            (rates_hbm, rates), (dest_hbm, dest_s), (dest_hbm, dest_v),
            (flags_hbm, flags_v), (links_hbm, links_v),
        ))
    ]
    for c in small:
        c.start()
    own = pltpu.make_async_copy(pop_hbm, near, own_sem.at[5])
    own.start()

    def copy(i, src, dst, target):
        return pltpu.make_async_remote_copy(
            src_ref=src, dst_ref=dst, send_sem=send.at[i], recv_sem=recv.at[i],
            device_id=(target,), device_id_type=MESH,
        )

    up_meta = [
        copy(0, dest_hbm, dest_low, me + 1),
        copy(1, links_hbm, links_low, me + 1),
        copy(2, flags_hbm, flags_low, me + 1),
    ]
    down_meta = [
        copy(3, links_hbm, links_high, me - 1),
        copy(4, flags_hbm, flags_high, me - 1),
    ]
    up_pop = [
        copy(
            5 + i, pop_hbm.at[:, pl.ds(held - span_low + i * CHUNK, CHUNK)],
            low.at[:, pl.ds(i * CHUNK, CHUNK)], me + 1,
        )
        for i in range(span_low // CHUNK)
    ]
    down_pop = [
        copy(
            8 + i, pop_hbm.at[:, pl.ds(i * CHUNK, CHUNK)],
            high.at[:, pl.ds(i * CHUNK, CHUNK)], me - 1,
        )
        for i in range(span_high // CHUNK)
    ]
    ups, downs = up_meta + up_pop, down_meta + down_pop

    @pl.when(has_low & has_high)
    def _():
        pl.semaphore_wait(barrier, 2)

    @pl.when(jnp.logical_not(has_low & has_high))
    def _():
        pl.semaphore_wait(barrier, 1)

    @pl.when(has_high)
    def _():
        for c in ups:
            c.start()

    @pl.when(has_low)
    def _():
        for c in downs:
            c.start()

    @pl.when(jnp.logical_not(has_low))
    def _():
        low[...] = jnp.zeros_like(low)
        flags_low[...] = jnp.zeros_like(flags_low)
        links_low[...] = jnp.zeros_like(links_low)
        dest_low[...] = jnp.zeros_like(dest_low)

    @pl.when(jnp.logical_not(has_high))
    def _():
        high[...] = jnp.zeros_like(high)
        flags_high[...] = jnp.zeros_like(flags_high)
        links_high[...] = jnp.zeros_like(links_high)

    for c in small:
        c.wait()
    scale = [rates[0, k] * (1.0 / NORMS[k]) for k in range(19)]

    def settle(load, kind_at, row, store):
        f = [load(q) for q in range(19)]
        g = collide(f, kind_at, lambda k: scale[k])
        for q in range(19):
            store(q, row, g[q])

    def keep(q, row, value):
        if q > 0:
            high_part = value.astype(jnp.bfloat16)
            low_part = (value - high_part.astype(jnp.float32)).astype(jnp.bfloat16)
            split[q - 1, pl.ds(row, CHUNK), 0:SITES] = high_part
            split[q - 1, pl.ds(row, CHUNK), SITES : 2 * SITES] = low_part

    @pl.when(has_low)
    def _():
        for c in up_meta:
            c.wait_recv()

    @pl.when(has_high)
    def _():
        for c in down_meta:
            c.wait_recv()

    came = dest_v[0:1, 0:1] - me * cap
    came_low = dest_low[0:1, 0:1] - (me - 1) * cap
    gone = jnp.sum(
        jnp.where(dest_v[...] >= (me + 1) * cap, 1.0, 0.0), axis=1, keepdims=True
    ).astype(jnp.int32)

    base_low = held * -1 + span_low - came_low
    base_own = span_low - came
    base_high = span_low + held - gone
    lane_slot = lax.broadcasted_iota(jnp.int32, (1, cap), 1)
    pos_low = base_low + lane_slot
    pos_own = base_own + lane_slot
    pos_high = base_high + lane_slot
    pos_low = jnp.where((pos_low < base_own) & has_low, pos_low, -1)
    pos_own = jnp.where(pos_own < base_high, pos_own, -1)
    pos_high = jnp.where(has_high, pos_high, -1)
    row_id = lax.broadcasted_iota(jnp.int32, (rows, cap), 0)
    picks = [
        jnp.where(row_id == p, 1.0, 0.0).astype(jnp.bfloat16) for p in (pos_low, pos_own, pos_high)
    ]
    total = None
    for pick, ref in zip(picks, (flags_low, flags_v, flags_high)):
        part = jnp.dot(
            pick, ref[...].astype(jnp.float32).astype(jnp.bfloat16),
            preferred_element_type=jnp.float32,
        )
        total = part if total is None else total + part
    kinds[...] = (total + 0.5).astype(jnp.int32)

    total = None
    for pick, ref in zip(picks, (links_low, links_v, links_high)):
        link = ref[...]
        where = jnp.where(
            link >= (me + 1) * cap, base_high + (link - (me + 1) * cap),
            jnp.where(link >= me * cap, base_own + (link - me * cap), base_low + (link - (me - 1) * cap)),
        )
        where = jnp.where((link >= 0) & (where >= 0) & (where < rows), where + 1, 0)
        part = lax.dot_general(
            pick[LAYER : LAYER + inner], where.astype(jnp.float32).astype(jnp.bfloat16),
            (((1,), (1,)), ((), ())), preferred_element_type=jnp.float32,
        )
        total = part if total is None else total + part
    reach[...] = total
    source_id = lax.broadcasted_iota(jnp.int32, (inner, rows), 1).astype(jnp.float32) + 1.0
    for d in range(18):
        column = jnp.broadcast_to(reach[:, d : d + 1], (inner, rows))
        hops[d] = jnp.where(column == source_id, 1.0, 0.0).astype(jnp.bfloat16)

    own.wait()

    def first(ref, base, start, count):
        def step(i, carry):
            at = pl.multiple_of(start + i * CHUNK, CHUNK)
            row = pl.multiple_of(base + at, CHUNK)

            def store(q, row, value):
                keep(q, row, value)
                ref[q, pl.ds(at, CHUNK), :] = value

            settle(lambda q: ref[q, pl.ds(at, CHUNK), :], kinds[pl.ds(row, CHUNK), :], row, store)
            return carry

        lax.fori_loop(0, count // CHUNK, step, 0)

    first(near, span_low, 0, held)

    def arrive_low(i):
        @pl.when(has_low)
        def _():
            up_pop[i].wait_recv()

        first(low, 0, i * CHUNK, CHUNK)

    def arrive_high(i):
        @pl.when(has_high)
        def _():
            down_pop[i].wait_recv()

        first(high, span_low + held, i * CHUNK, CHUNK)

    arrive_low(0)
    arrive_high(0)
    arrive_low(1)
    arrive_high(1)
    arrive_low(2)

    def stream(q, own_q, own_opp, lo, count):
        lane = lax.broadcasted_iota(jnp.int32, (count, SITES), 1)
        cx, cy, cz = VELOCITIES[q]
        moved = rolled(own_q, 32 * cx + 8 * cy + cz)
        value = jnp.where(lane_region(q, (0, 0, 0), lane), moved, own_opp)
        entries = regions_of(q)
        picks = [hops[d, lo : lo + count, :] for d, _, _ in entries]
        pick = picks[0] if len(picks) == 1 else jnp.concatenate(picks, axis=0)
        got = jnp.dot(pick, split[q - 1], preferred_element_type=jnp.float32)
        got = got[:, 0:SITES] + got[:, SITES : 2 * SITES]
        for i, (d, step, shift) in enumerate(entries):
            present = jnp.broadcast_to(reach[lo : lo + count, d : d + 1], (count, SITES)) > 0.0
            use = jnp.logical_and(lane_region(q, step, lane), present)
            value = jnp.where(use, rolled(got[i * count : (i + 1) * count], shift), value)
        return value

    def whole(q):
        return jnp.concatenate(
            [low[q, LAYER:span_low, :], near[q], high[q, 0:LAYER, :]], axis=0
        )

    second[0] = whole(0)
    for q in range(1, 19):
        second[q] = stream(q, whole(q), whole(19 - q), 0, inner)

    def again(i, carry):
        at = pl.multiple_of(i * CHUNK, CHUNK)
        row = pl.multiple_of(at + LAYER, CHUNK)

        def store(q, row, value):
            keep(q, row, value)
            second[q, pl.ds(at, CHUNK), :] = value

        settle(lambda q: second[q, pl.ds(at, CHUNK), :], kinds[pl.ds(row, CHUNK), :], row, store)
        return carry

    lax.fori_loop(0, inner // CHUNK, again, 0)

    row_of = lax.broadcasted_iota(jnp.int32, (final, SITES), 0)
    full = row_of < final - gone
    skip = jnp.clip(LAYER - (dest_s[0, 0] - me * cap), 0, LAYER)
    for q in range(19):
        if q == 0:
            value = second[0, LAYER : LAYER + final, :]
        else:
            value = stream(
                q, second[q, LAYER : LAYER + final, :], second[19 - q, LAYER : LAYER + final, :],
                LAYER, final,
            )
        result[q, 0:final, :] = jnp.where(full, value, 0.0)
        result[q, final : final + LAYER, :] = jnp.zeros((LAYER, SITES), jnp.float32)
        out[q] = result[q, pl.ds(skip, cap), :]

    @pl.when(has_high)
    def _():
        for c in ups:
            c.wait_send()

    @pl.when(has_low)
    def _():
        for c in downs:
            c.wait_send()


def local(populations, relax_rates, destination, block_links, site_flags):
    n = lax.axis_size("blk")
    held, cap = populations.shape[0], site_flags.shape[0]
    rows = held + 5 * LAYER
    inner, final = rows - 2 * LAYER, held + LAYER
    f32, i32 = jnp.float32, jnp.int32
    out = pl.pallas_call(
        functools.partial(kernel, n, held, cap),
        out_shape=jax.ShapeDtypeStruct((Q, cap, SITES), f32),
        in_specs=[pl.BlockSpec(memory_space=pl.ANY)] * 5,
        out_specs=pl.BlockSpec(memory_space=pltpu.VMEM),
        scratch_shapes=[
            pltpu.VMEM((Q, held, SITES), f32),
            pltpu.VMEM((Q, 3 * LAYER, SITES), f32),
            pltpu.VMEM((Q, 2 * LAYER, SITES), f32),
            pltpu.VMEM((cap, SITES), i32),
            pltpu.VMEM((cap, SITES), i32),
            pltpu.VMEM((18, cap), i32),
            pltpu.VMEM((18, cap), i32),
            pltpu.VMEM((1, held), i32),
            pltpu.VMEM((rows, SITES), i32),
            pltpu.VMEM((inner, 18), f32),
            pltpu.VMEM((18, inner, rows), jnp.bfloat16),
            pltpu.VMEM((18, rows, 2 * SITES), jnp.bfloat16),
            pltpu.VMEM((Q, inner, SITES), f32),
            pltpu.VMEM((Q, final + LAYER, SITES), f32),
            pltpu.SMEM((1, 19), f32),
            pltpu.SMEM((1, held), i32),
            pltpu.VMEM((1, held), i32),
            pltpu.VMEM((cap, SITES), i32),
            pltpu.VMEM((18, cap), i32),
            pltpu.SemaphoreType.DMA((10,)),
            pltpu.SemaphoreType.DMA((10,)),
            pltpu.SemaphoreType.DMA((6,)),
        ],
        compiler_params=pltpu.CompilerParams(
            collective_id=0, has_side_effects=True, vmem_limit_bytes=62 * 1024 * 1024
        ),
    )(
        jnp.transpose(populations, (1, 0, 2)), relax_rates.reshape(1, Q),
        destination.reshape(1, held), site_flags, jnp.transpose(block_links, (1, 0)),
    )
    return jnp.transpose(out, (1, 0, 2))


def solution(mesh):
    in_specs = (P("blk", None, None), P(), P("blk"), P("blk", None), P("blk", None))
    out_specs = P("blk", None, None)
    return jax.shard_map(local, mesh=mesh, in_specs=in_specs, out_specs=out_specs, check_vma=False)
```
